32 devices in a mesh: wide: 8 (over y, x, core), narrow: 4 (over z).
Axes of the slice: x: 2, y: 2, z: 4, core: 2. Of those that a mesh axis runs over, the one named last changes fastest.
Arguments:
- tokens: bfloat16 [8192, 768], P('wide'), may hold values from -6 to 6
- segments: int32 [32, 256], P('wide'), may hold values from 0 to 1, never falling along the last dimension, each value on 1 to 200 neighbouring positions
- question: int32 [32], P('wide'), may hold values from 0 to 1, as said below
- answer_ids: int32 [2, 20], replicated, may hold values from 0 to 32127
- vocab_table: bfloat16 [32128, 768], P('wide'), may hold values from -6 to 6
- enc_gains: float32 [3, 768], replicated, may hold values from 0.5 to 1.5
- enc_inward: bfloat16 [768, 3, 768], P(None, None, 'narrow'), may hold values from -0.109375 to 0.109375
- encoder_bias: float32 [32, 12], P(None, 'narrow'), may hold values from -4 to 4
- enc_outward: bfloat16 [768, 768], P('narrow'), may hold values from -1.75 to 1.75
- enc_grow: bfloat16 [768, 3072], P(None, 'narrow'), may hold values from -0.21875 to 0.21875
- enc_shrink: bfloat16 [3072, 768], P('narrow'), may hold values from -0.109375 to 0.109375
- cross_key_value_weight: bfloat16 [768, 2, 768], P(None, None, 'narrow'), may hold values from -0.109375 to 0.109375
- dec_gains: float32 [3, 768], replicated, may hold values from 0.5 to 1.5
- dec_inward: bfloat16 [768, 3, 768], P(None, None, 'narrow'), may hold values from -0.109375 to 0.109375
- decoder_bias: float32 [32, 12], P(None, 'narrow'), may hold values from -4 to 4
- dec_outward: bfloat16 [768, 768], P('narrow'), may hold values from -1.75 to 1.75
- cross_query: bfloat16 [768, 768], P(None, 'narrow'), may hold values from -0.109375 to 0.109375
- cross_outward: bfloat16 [768, 768], P('narrow'), may hold values from -2.5 to 2.5
- dec_grow: bfloat16 [768, 3072], P(None, 'narrow'), may hold values from -0.21875 to 0.21875
- dec_shrink: bfloat16 [3072, 768], P('narrow'), may hold values from -0.109375 to 0.109375
- grad_memory: bfloat16 [8192, 768], P('wide'), may hold values from -6 to 6
- grad_output: bfloat16 [40, 768], replicated, may hold values from -6 to 6
Outputs:
- memory: bfloat16 [8192, 768], P('wide')
- output: bfloat16 [40, 768], replicated
- grad_tokens: bfloat16 [8192, 768], P('wide')
- grad_vocab_table: float32 [32128, 768], P('wide')
- grad_enc_gains: float32 [3, 768], replicated
- grad_enc_inward: float32 [768, 3, 768], P('wide', None, 'narrow')
- grad_enc_bias: float32 [32, 12], P(None, 'narrow')
- grad_enc_outward: float32 [768, 768], P('narrow', 'wide')
- grad_enc_grow: float32 [768, 3072], P('wide', 'narrow')
- grad_enc_shrink: float32 [3072, 768], P('narrow', 'wide')
- grad_cross_inward: float32 [768, 2, 768], P('wide', None, 'narrow')
- grad_dec_gains: float32 [3, 768], replicated
- grad_dec_inward: float32 [768, 3, 768], P(None, None, 'narrow')
- gradient_decoder_bias: float32 [32, 12], P(None, 'narrow')
- grad_dec_outward: float32 [768, 768], P('narrow')
- grad_cross_query: float32 [768, 768], P(None, 'narrow')
- grad_cross_outward: float32 [768, 768], P('narrow')
- grad_dec_grow: float32 [768, 3072], P(None, 'narrow')
- grad_dec_shrink: float32 [3072, 768], P('narrow')
The draws below stay inside these ranges and needn't reach their ends.
Inputs may be any that keep to these rules, and one draw needn't show every extreme that they name: `segments`: along each row the passage ids never fall; each passage holds 1 to 200 tokens. Each aligned block of 2 rows holds every question id once, so every question owns exactly 16 rows; the first row's question also owns the last row.
All inputs are finite; a program needn't handle non-finite values.
Results may differ from the reference program's by a relative error of at most 0.024.
The reference program's roundings to bfloat16 on the way count: a program that leaves them out, or rounds other values in their place, can miss the bound.
Values may be sent and summed in bfloat16 or wider, within the bound.
No kernel may reach another device: no remote copies, remote signals or barrier semaphores. Data moves between devices by JAX's collectives and lax.ppermute only.
A program may use at most 192 MiB of HBM per device.

```python
import math
import jax
import jax.numpy as jnp
import numpy as np
from jax import lax

D = 768
H = 12
HD = 64
FF = 3072
VOCAB = 32128
POSITION_BUCKETS = 32
ROW_LEN = 256
PASSAGES = 2
PASSAGE_MOST = 200
ANSWER_TOKENS = 20
ROWS = 32
TOKENS = 8192
QUESTIONS = 2
DEC = 40
INNER = 768


def draw_question(key, part):
    block_count = ROWS // QUESTIONS
    block_keys = jax.random.split(jax.random.fold_in(key, 7), block_count)
    orders = jax.vmap(lambda one_key: jax.random.permutation(one_key, QUESTIONS))(block_keys).astype(jnp.int32)
    orders = orders.at[block_count - 1].set(orders[0][::-1])
    return orders.reshape(-1).astype(jnp.int32)


def touch_ends(array, stream_key, least, largest):
    longest = array.shape.index(max(array.shape))
    spots = []
    for shift in (0, 1):
        where = [jax.random.randint(jax.random.fold_in(stream_key, axis), (), 0, length) for axis, length in enumerate(array.shape)]
        where[longest] = (where[longest] + shift) % array.shape[longest]
        spots.append(tuple(where))
    return array.at[spots[0]].set(least).at[spots[1]].set(largest)


def with_spikes(entries, stream_key, source, target, parts, factor):
    def block_of(axis_at):
        return (jnp.arange(entries.shape[axis_at]) // (entries.shape[axis_at] // parts)).reshape((-1,) + (1,) * (entries.ndim - 1 - axis_at))

    one_side = jax.random.permutation(stream_key, parts)[block_of(target)]
    second = (block_of(target) + parts // 2) % parts
    return jnp.where((block_of(source) == one_side) | (block_of(source) == second), factor * entries, entries)


def levels(rng, dims, cuts, smallest, top_value):
    def one(axis_at, parts):
        heights = jax.random.uniform(jax.random.fold_in(jax.random.fold_in(rng, 6), axis_at), (parts,), jnp.float32, smallest / len(cuts), top_value / len(cuts))
        return jnp.repeat(jnp.exp(heights), dims[axis_at] // parts).reshape((-1,) + (1,) * (len(dims) - axis_at - 1))

    level = one(*cuts[0])
    for cut in cuts[1:]:
        level = level * one(*cut)
    return level


def cumulative_ranks(count, lean):
    portions = [(1 << 20) // math.isqrt(grade ** lean) + 1 for grade in range(1, count + 1)]
    scale = 1 + sum(portions) // (1 << 30)
    return np.cumsum(np.array([max(1, weight // scale) for weight in portions]))


def ranked_ids(own_key, dims, count, lean):
    listing = cumulative_ranks(count, lean)
    lot = jax.random.randint(jax.random.fold_in(own_key, 1), dims, 0, int(listing[count - 1]))
    grade = jnp.searchsorted(jnp.asarray(listing, jnp.int32), lot, side="right")
    return jax.random.permutation(jax.random.fold_in(own_key, 2), count)[grade].astype(jnp.int32)


def profile(count, total, reach, slope):
    portions = [(1 << 20) // math.isqrt(standing ** slope) + 1 for standing in range(2, count + 1)]
    spare, given = total - reach - (count - 1), [1] * (count - 1)
    while spare > 0:
        candidates = [i for i in range(count - 1) if given[i] < reach]
        whole, left = sum([portions[i] for i in candidates]), spare
        for i in candidates:
            extra = min(reach - given[i], max(1, left * portions[i] // whole), spare)
            given[i] = given[i] + extra
            spare = spare - extra
    return np.array([reach] + given)


def uneven_parts(own_key, count, total, limit, slope):
    if count == 2:
        one = jax.random.randint(own_key, (), max(1, total - limit), min(limit, total - 1) + 1)
        return jnp.stack([one, total - one])
    tallies = jnp.asarray(profile(count, total, limit, slope), jnp.int32)
    pairs = (count - 1) // 2
    giver, receiver = tallies[1:1 + 2 * pairs:2], tallies[2:2 + 2 * pairs:2]
    margin = jnp.minimum(giver - 1, limit - receiver)
    shifted = jax.random.randint(jax.random.fold_in(own_key, 1), (pairs,), 0, 1 << 20) % (margin + 1)
    tallies = tallies.at[1:1 + 2 * pairs:2].set(giver - shifted).at[2:2 + 2 * pairs:2].set(receiver + shifted)
    return tallies[jax.random.permutation(jax.random.fold_in(own_key, 2), count)]


def normal_values(key, extent, scale, reach, pieces=(), kind=jnp.bfloat16):
    array = scale * jax.random.normal(key, extent, jnp.float32)
    if pieces:
        array = array * levels(key, extent, pieces, -0.22, 0.18)
    return jnp.clip(array, -reach, reach).astype(kind)


def gaussian_with(rng, extent, scale, bound, pieces, heavy, kind=jnp.bfloat16):
    entries = scale * jax.random.normal(rng, extent, jnp.float32)
    if pieces:
        entries = entries * levels(rng, extent, pieces, -0.22, 0.18)
    return jnp.clip(with_spikes(entries, jax.random.fold_in(rng, 3), *heavy), -bound, bound).astype(kind)


def setup_inputs(seed: int = 0) -> dict:
    splits = jax.random.split(jax.random.key(seed), 23)
    tokens = gaussian_with(splits[0], (TOKENS, D), 1.0, 6.0, ((0, 8),), (0, 1, 8, 2.0))
    segments = jax.vmap(lambda own: jnp.searchsorted(jnp.cumsum(uneven_parts(own, PASSAGES, ROW_LEN, PASSAGE_MOST, 1)), jnp.arange(ROW_LEN), side="right"))(jax.random.split(splits[1], ROWS)).reshape((ROWS, ROW_LEN)).astype(jnp.int32)
    question = draw_question(jax.random.fold_in(splits[22], 71), 0)
    answer_ids = touch_ends(ranked_ids(splits[3], (QUESTIONS, ANSWER_TOKENS), VOCAB, 2), jax.random.fold_in(splits[3], 3), 0, VOCAB - 1).astype(jnp.int32)
    vocab_table = normal_values(splits[4], (VOCAB, D), 1.0, 6.0, ((0, 8),))
    enc_gains = jnp.clip(1.0 + 0.1 * jax.random.normal(splits[5], (3, D), jnp.float32), 0.5, 1.5)
    enc_inward = normal_values(splits[6], (D, 3, INNER), (4 * D) ** -0.5, 0.109375, ((2, 4),))
    encoder_bias = normal_values(splits[7], (POSITION_BUCKETS, H), 1.0, 4.0, ((1, 4),), jnp.float32)
    enc_outward = normal_values(splits[8], (INNER, D), (D // 64) ** -0.5, 1.75, ((0, 4),))
    enc_grow = normal_values(splits[9], (D, FF), D ** -0.5, 0.21875, ((1, 4),))
    enc_shrink = normal_values(splits[10], (FF, D), FF ** -0.5, 0.109375, ((0, 4),))
    cross_key_value_weight = normal_values(splits[11], (D, 2, INNER), (4 * D) ** -0.5, 0.109375, ((2, 4),))
    dec_gains = jnp.clip(1.0 + 0.1 * jax.random.normal(splits[12], (3, D), jnp.float32), 0.5, 1.5)
    dec_inward = normal_values(splits[13], (D, 3, INNER), (4 * D) ** -0.5, 0.109375, ((2, 4),))
    decoder_bias = normal_values(splits[14], (POSITION_BUCKETS, H), 1.0, 4.0, ((1, 4),), jnp.float32)
    dec_outward = normal_values(splits[15], (INNER, D), (D // 64) ** -0.5, 1.75, ((0, 4),))
    cross_query = normal_values(splits[16], (D, INNER), (4 * D) ** -0.5, 0.109375, ((1, 4),))
    cross_outward = normal_values(splits[17], (INNER, D), (max(1, D // 128)) ** -0.5, 2.5, ((0, 4),))
    dec_grow = normal_values(splits[18], (D, FF), D ** -0.5, 0.21875, ((1, 4),))
    dec_shrink = normal_values(splits[19], (FF, D), FF ** -0.5, 0.109375, ((0, 4),))
    grad_memory = gaussian_with(splits[20], (TOKENS, D), 1.0, 6.0, ((0, 8),), (0, 1, 8, 2.0))
    grad_output = normal_values(splits[21], (DEC, D), 1.0, 6.0)
    return {"tokens": tokens, "segments": segments, "question": question, "answer_ids": answer_ids, "vocab_table": vocab_table, "enc_gains": enc_gains, "enc_inward": enc_inward, "encoder_bias": encoder_bias, "enc_outward": enc_outward, "enc_grow": enc_grow, "enc_shrink": enc_shrink, "cross_key_value_weight": cross_key_value_weight, "dec_gains": dec_gains, "dec_inward": dec_inward, "decoder_bias": decoder_bias, "dec_outward": dec_outward, "cross_query": cross_query, "cross_outward": cross_outward, "dec_grow": dec_grow, "dec_shrink": dec_shrink, "grad_memory": grad_memory, "grad_output": grad_output}


EPSILON = 1e-06
BOTH_EDGES = (12, 16, 23, 32, 46, 64, 91)
CAUSAL_EDGES = (19, 21, 24, 27, 31, 35, 40, 46, 52, 59, 67, 77, 87, 99, 113)
PRECISION_FULL = lax.Precision.HIGHEST
MASKED = -1e+30

@jax.custom_vjp
def low(v):
    return lax.optimization_barrier(v.astype(jnp.bfloat16)).astype(jnp.float32)

@jax.custom_vjp
def low_back(v):
    return v

def low_keep(v):
    return (low(v), None)

def low_pass(kept, grad):
    return (grad,)

def back_keep(v):
    return (v, None)

def back_low(kept, grad):
    return (low(grad),)
low.defvjp(low_keep, low_pass)
low_back.defvjp(back_keep, back_low)

def bucket_both(length):
    places = jnp.arange(length, dtype=jnp.int32)
    offset = places[None, :] - places[:, None]
    spread = jnp.abs(offset)
    far_bucket = 8 + sum(((spread >= border).astype(jnp.int32) for border in BOTH_EDGES))
    near = jnp.where(spread < 8, spread, far_bucket)
    return (jnp.where(offset > 0, 16, 0) + near).astype(jnp.int32)

def causal_bucket_ids(length):
    places = jnp.arange(length, dtype=jnp.int32)
    spread = jnp.maximum(places[:, None] - places[None, :], 0)
    far_bucket = 16 + sum(((spread >= border).astype(jnp.int32) for border in CAUSAL_EDGES))
    return jnp.where(spread < 16, spread, far_bucket).astype(jnp.int32)

def bucket_lookup(buckets, bucket_count):
    return (jnp.arange(bucket_count, dtype=jnp.int32)[:, None, None] == buckets[None]).astype(jnp.float32)

def norm_rows(values, gain_row):
    return values * lax.rsqrt(lax.optimization_barrier(jnp.mean(values * values, axis=-1, keepdims=True)) + EPSILON) * gain_row

def attend(normalized_rows, input_weight, outward, expanded_bias, allowed):
    row_total, length = (normalized_rows.shape[0], normalized_rows.shape[1])
    projection_output = low(low_back(jnp.einsum('weq,qyb->yweb', normalized_rows, input_weight, precision=PRECISION_FULL)))
    head_split = projection_output.reshape(3, row_total, length, H, HD)
    scores = jnp.einsum('rqhe,rkhe->rhqk', head_split[0], head_split[1], precision=PRECISION_FULL) + expanded_bias[None]
    scores = low_back(scores)
    masked = jnp.where(allowed, scores, MASKED)
    highest = lax.optimization_barrier(jnp.max(masked, axis=-1, keepdims=True))
    exponent = jnp.exp(masked - highest)
    weights = low(exponent / lax.optimization_barrier(jnp.sum(exponent, axis=-1, keepdims=True)))
    context = jnp.einsum('rhqk,rkhe->rqhe', weights, head_split[2], precision=PRECISION_FULL)
    context = low(low_back(context.reshape(row_total, length, H * HD)))
    return low_back(jnp.einsum('rli,id->rld', context, outward, precision=PRECISION_FULL))

def feed_forward(normalized_rows, grow_weight, shrink_weight):
    grown_rows = low_back(jnp.einsum('...d,df->...f', normalized_rows, grow_weight, precision=PRECISION_FULL))
    activated = low(jax.nn.gelu(grown_rows, approximate=True))
    return low_back(jnp.einsum('...f,fd->...d', activated, shrink_weight, precision=PRECISION_FULL))

def encoder_rows(row_block, enc_weights):
    rows_in, seg_rows = row_block
    enc_gains, enc_inward, encoder_bias, enc_outward, enc_grow, enc_shrink = enc_weights
    bucket_indicator_table = bucket_lookup(bucket_both(ROW_LEN), POSITION_BUCKETS)
    expanded_bias = jnp.einsum('uxe,uc->cxe', bucket_indicator_table, encoder_bias, precision=PRECISION_FULL)
    allowed = (seg_rows[:, :, None] == seg_rows[:, None, :])[:, None]
    hidden = rows_in + attend(low(norm_rows(rows_in, enc_gains[0])), enc_inward, enc_outward, expanded_bias, allowed)
    summed = hidden + feed_forward(low(norm_rows(hidden, enc_gains[1])), enc_grow, enc_shrink)
    return low(norm_rows(summed, enc_gains[2]))

def forward(tokens, vocab_table, enc_gains, enc_inward, encoder_bias, enc_outward, enc_grow, enc_shrink, cross_key_value_weight, dec_gains, dec_inward, decoder_bias, dec_outward, cross_query, cross_outward, dec_grow, dec_shrink, segments, question, answer_ids):
    block_rows = math.gcd(ROWS, 16)
    block_count = ROWS // block_rows
    rows_all = tokens.reshape(block_count, block_rows, ROW_LEN, D)
    seg_all = segments.reshape(block_count, block_rows, ROW_LEN)
    enc_weights = (enc_gains, enc_inward, encoder_bias, enc_outward, enc_grow, enc_shrink)

    def one_block(row_block):
        return encoder_rows(row_block, enc_weights)
    memory = lax.map(jax.checkpoint(one_block), (rows_all, seg_all)).reshape(TOKENS, D)
    embedded = vocab_table[answer_ids.reshape(-1)]
    places = jnp.arange(ANSWER_TOKENS, dtype=jnp.int32)
    causal = (places[:, None] >= places[None, :])[None, None]
    decoder_bias_expanded = jnp.einsum('uxe,uc->cxe', bucket_lookup(causal_bucket_ids(ANSWER_TOKENS), POSITION_BUCKETS), decoder_bias, precision=PRECISION_FULL)
    dec_rows = embedded.reshape(QUESTIONS, ANSWER_TOKENS, D)
    first = dec_rows + attend(low(norm_rows(dec_rows, dec_gains[0])), dec_inward, dec_outward, decoder_bias_expanded, causal)
    first = first.reshape(DEC, D)
    queries = low(low_back(jnp.dot(low(norm_rows(first, dec_gains[1])), cross_query, precision=PRECISION_FULL)))
    stacked_key_value = low(low_back(jnp.einsum('yo,ovw->vyw', memory, cross_key_value_weight, precision=PRECISION_FULL)))
    dec_question = jnp.arange(DEC, dtype=jnp.int32) // ANSWER_TOKENS
    token_question = jnp.repeat(question, ROW_LEN)
    cross_allowed = dec_question[:, None] == token_question[None, :]

    def cross_head(head_parts):
        query_rows, key_rows, value_rows = head_parts
        scores = low_back(jnp.dot(query_rows, key_rows.T, precision=PRECISION_FULL))
        masked = jnp.where(cross_allowed, scores, MASKED)
        highest = lax.optimization_barrier(jnp.max(masked, axis=-1, keepdims=True))
        logsum = highest + jnp.log(lax.optimization_barrier(jnp.sum(jnp.exp(masked - highest), axis=-1, keepdims=True)))
        return jnp.dot(low(jnp.exp(masked - logsum)), value_rows, precision=PRECISION_FULL)
    query_heads = queries.reshape(DEC, H, HD).transpose(1, 0, 2)
    key_heads = stacked_key_value[0].reshape(TOKENS, H, HD).transpose(1, 0, 2)
    value_heads = stacked_key_value[1].reshape(TOKENS, H, HD).transpose(1, 0, 2)
    context = lax.map(jax.checkpoint(cross_head), (query_heads, key_heads, value_heads))
    context = low(low_back(context.transpose(1, 0, 2).reshape(DEC, H * HD)))
    second = first + low_back(jnp.dot(context, cross_outward, precision=PRECISION_FULL))
    output = second + feed_forward(low(norm_rows(second, dec_gains[2])), dec_grow, dec_shrink)
    return (memory, output)

def reference(tokens, segments, question, answer_ids, vocab_table, enc_gains, enc_inward, encoder_bias, enc_outward, enc_grow, enc_shrink, cross_key_value_weight, dec_gains, dec_inward, decoder_bias, dec_outward, cross_query, cross_outward, dec_grow, dec_shrink, grad_memory, grad_output):
    floats = tuple((operand.astype(jnp.float32) for operand in (tokens, vocab_table, enc_gains, enc_inward, encoder_bias, enc_outward, enc_grow, enc_shrink, cross_key_value_weight, dec_gains, dec_inward, decoder_bias, dec_outward, cross_query, cross_outward, dec_grow, dec_shrink)))

    def forward_all(*params):
        return forward(*params, segments, question, answer_ids)
    (memory, output), pullback = jax.vjp(forward_all, *floats)
    gradients = pullback((grad_memory.astype(jnp.float32), grad_output.astype(jnp.float32)))
    return (memory.astype(jnp.bfloat16), output.astype(jnp.bfloat16), gradients[0].astype(jnp.bfloat16), gradients[1], gradients[2], gradients[3], gradients[4], gradients[5], gradients[6], gradients[7], gradients[8], gradients[9], gradients[10], gradients[11], gradients[12], gradients[13], gradients[14], gradients[15], gradients[16])
```

```python
import jax
import jax.numpy as jnp
from jax import lax
from jax.experimental import pallas as pl
from jax.experimental.pallas import tpu as pltpu
from jax.sharding import PartitionSpec as P

HD = 64
EPSILON = 1e-06
BOTH_EDGES = (12, 16, 23, 32, 46, 64, 91)
CAUSAL_EDGES = (19, 21, 24, 27, 31, 35, 40, 46, 52, 59, 67, 77, 87, 99, 113)
FULL = lax.Precision.HIGHEST
F32 = jnp.float32
BF16 = jnp.bfloat16
MASKED = -1e30


def bits_of(count):
    return [1 << k for k in range(count.bit_length() - 1)]


def swap(value, axis, bit):
    count = lax.axis_size(axis)
    pairs = [(i, i ^ bit) for i in range(count)]
    return jax.tree.map(lambda part: lax.ppermute(part, axis, pairs), value)


def exchange_sum(value, axis):
    for bit in bits_of(lax.axis_size(axis)):
        value = jax.tree.map(jnp.add, value, swap(value, axis, bit))
    return value


def rounded_sum(*parts):
    return sum(part.astype(F32) for part in parts).astype(BF16)


def place(starts, jobs, shape):
    arrays = [array for array, _ in jobs]

    def kernel(starts_ref, *refs):
        pieces, out, sem = refs[: len(arrays)], refs[len(arrays)], refs[len(arrays) + 1]
        copies = []
        for piece, (_, targets) in zip(pieces, jobs):
            for source, index, first, rows in targets:
                z, w = starts_ref[index, 0], starts_ref[index, 1]
                if source is None:
                    copies.append((piece, out.at[z]))
                else:
                    copies.append((piece.at[source], out.at[z, w, pl.ds(first, rows)]))
        for number, (source, target) in enumerate(copies):
            pltpu.make_async_copy(source, target, sem.at[number]).start()
        for number, (source, target) in enumerate(copies):
            pltpu.make_async_copy(source, target, sem.at[number]).wait()

    count = sum(len(targets) for _, targets in jobs)
    return pl.pallas_call(
        kernel,
        out_shape=jax.ShapeDtypeStruct(shape, arrays[0].dtype),
        grid_spec=pltpu.PrefetchScalarGridSpec(
            num_scalar_prefetch=1,
            in_specs=[pl.BlockSpec(memory_space=pl.ANY)] * len(arrays),
            out_specs=pl.BlockSpec(memory_space=pl.ANY),
            grid=(1,),
            scratch_shapes=[pltpu.SemaphoreType.DMA((count,))],
        ),
    )(starts, *arrays)


def gather_weights(quarter):
    blocks, rows, lanes = quarter.shape
    parts = lax.axis_size("narrow")
    wide_at, narrow_at = lax.axis_index("wide"), lax.axis_index("narrow")
    mine = lax.dynamic_index_in_dim(quarter, wide_at, 0, keepdims=False)
    others = jnp.stack([swap(mine, "narrow", offset) for offset in range(1, parts)])
    pieces = [(0, 0, others)]
    bits = bits_of(blocks)[::-1]
    if len(bits) >= 3 and rows % 32 == 0:
        a, b = bits[:2]
        half = rows // 2
        over_a, over_b = swap(others, "wide", a), swap(others, "wide", b)
        far_a = swap(over_b[:, :half], "wide", a)
        far_b = swap(over_a[:, half:], "wide", b)
        pieces += [(a, 0, over_a), (b, 0, over_b), (a ^ b, 0, far_a), (a ^ b, half, far_b)]
        bits = bits[2:]
    for bit in bits:
        pieces += [(at ^ bit, first, swap(piece, "wide", bit)) for at, first, piece in pieces]
    jobs = [(quarter, [(None, 0, 0, rows)])]
    starts = [(narrow_at, jnp.int32(0))]
    for at, first, piece in pieces:
        targets = []
        for offset in range(1, parts):
            targets.append((offset - 1, len(starts), first, piece.shape[1]))
            starts.append((narrow_at ^ offset, wide_at ^ at))
        jobs.append((piece, targets))
    table = jnp.stack([jnp.stack(pair) for pair in starts]).astype(jnp.int32)
    return place(table, jobs, (parts, blocks, rows, lanes))


def scatter_sums(whole):
    parts, blocks, rows, lanes = whole.shape
    wide_at, narrow_at = lax.axis_index("wide"), lax.axis_index("narrow")

    def block(at):
        return lax.dynamic_index_in_dim(whole, wide_at ^ at, 1, keepdims=False)

    even = jnp.stack([block(at) for at in range(0, blocks, 2)])
    odd = jnp.stack([block(at) for at in range(1, blocks, 2)])
    held = rounded_sum(even, swap(odd, "wide", 1))
    bits = bits_of(blocks)[1:]
    if len(bits) == 2 and rows % 32 == 0:
        a, b = bits
        half = rows // 2
        far = held[3]
        from_a = swap(far[:, :half], "wide", a)
        from_b = swap(far[:, half:], "wide", b)
        send_b = jnp.concatenate([rounded_sum(held[2][:, :half], from_a), held[2][:, half:]], axis=1)
        send_a = jnp.concatenate([held[1][:, :half], rounded_sum(held[1][:, half:], from_b)], axis=1)
        total = rounded_sum(held[0], swap(send_a, "wide", a), swap(send_b, "wide", b))
    else:
        for bit in bits[::-1]:
            half = held.shape[0] // 2
            held = rounded_sum(held[:half], swap(held[half:], "wide", bit))
        total = held[0]

    def part(offset):
        return lax.dynamic_index_in_dim(total, narrow_at ^ offset, 0, keepdims=False)

    result = part(0).astype(F32)
    for offset in range(1, parts):
        result = result + swap(part(offset), "narrow", offset).astype(F32)
    return result


def spread_rows(mine):
    parts = lax.axis_size("narrow")
    narrow_at = lax.axis_index("narrow")
    whole = jnp.zeros((parts,) + mine.shape, mine.dtype)
    for offset in range(parts):
        piece = mine if offset == 0 else swap(mine, "narrow", offset)
        whole = lax.dynamic_update_index_in_dim(whole, piece, narrow_at ^ offset, 0)
    return whole.reshape((-1,) + mine.shape[1:])


def bucket_both(length):
    places = jnp.arange(length, dtype=jnp.int32)
    offset = places[None, :] - places[:, None]
    spread = jnp.abs(offset)
    far_bucket = 8 + sum(((spread >= border).astype(jnp.int32) for border in BOTH_EDGES))
    near = jnp.where(spread < 8, spread, far_bucket)
    return jnp.where(offset > 0, 16, 0) + near


def causal_bucket_ids(length):
    places = jnp.arange(length, dtype=jnp.int32)
    spread = jnp.maximum(places[:, None] - places[None, :], 0)
    far_bucket = 16 + sum(((spread >= border).astype(jnp.int32) for border in CAUSAL_EDGES))
    return jnp.where(spread < 16, spread, far_bucket)


def bucket_lookup(buckets, bucket_count):
    return (jnp.arange(bucket_count, dtype=jnp.int32)[:, None, None] == buckets[None]).astype(F32)


def smooth_gate(values):
    return jax.nn.gelu(values, approximate=True)


def smooth_gate_back(grown, upstream):
    _, pullback = jax.vjp(smooth_gate, grown)
    return pullback(upstream)[0]


def norm_rows(values, gain_row):
    inv_rms = lax.rsqrt(jnp.mean(values * values, axis=-1, keepdims=True) + EPSILON)
    return (values * inv_rms * gain_row, inv_rms)


def norm_back(gradient_normalized, values, inv_rms, gain_row):
    scaled = gradient_normalized * gain_row
    inv_cubed = inv_rms * inv_rms * inv_rms
    grad_values = inv_rms * scaled - values * inv_cubed * jnp.mean(
        scaled * values, axis=-1, keepdims=True
    )
    return (grad_values, gradient_normalized * values * inv_rms)


def dot(spec, left, right):
    return jnp.einsum(spec, left, right, preferred_element_type=F32)


def softmax_forward(queries, keys, values, bias, allowed):
    scores = dot("rqhe,rkhe->rhqk", queries, keys) + bias[None]
    masked = jnp.where(allowed, scores, MASKED)
    highest = jnp.max(masked, axis=-1, keepdims=True)
    exponent = jnp.exp(masked - highest)
    totals = jnp.sum(exponent, axis=-1, keepdims=True)
    weights = (exponent / totals).astype(BF16)
    context = dot("rhqk,rkhe->rqhe", weights, values).astype(BF16)
    return context, highest + jnp.log(totals)


def softmax_backward(queries, keys, values, bias, allowed, logsum, grad_context):
    scores = dot("rqhe,rkhe->rhqk", queries, keys) + bias[None]
    probs = jnp.exp(jnp.where(allowed, scores, MASKED) - logsum)
    grad_probs = dot("rqhe,rkhe->rhqk", grad_context, values)
    grad_values = dot("rhqk,rqhe->rkhe", probs.astype(BF16), grad_context)
    dot_term = jnp.sum(grad_probs * probs, axis=-1, keepdims=True)
    grad_scores = (probs * (grad_probs - dot_term)).astype(BF16)
    grad_queries = dot("rhqk,rkhe->rqhe", grad_scores, keys)
    grad_keys = dot("rhqk,rqhe->rkhe", grad_scores, queries)
    return [g.astype(BF16) for g in (grad_queries, grad_keys, grad_values)], jnp.sum(
        grad_scores.astype(F32), axis=0
    )


def merge_stats(first, second):
    first_max, first_total, first_sums = first
    second_max, second_total, second_sums = second
    ahead = first_max >= second_max
    high = jnp.where(ahead, first_max, second_max)
    scale = jnp.exp(jnp.where(ahead, second_max, first_max) - high)
    total = jnp.where(ahead, first_total, second_total) + scale * jnp.where(
        ahead, second_total, first_total
    )
    sums = jnp.where(ahead[..., None], first_sums, second_sums) + scale[..., None] * jnp.where(
        ahead[..., None], second_sums, first_sums
    )
    return high, total, sums


def per_device(
    tokens,
    segments,
    question,
    answer_ids,
    vocab_table,
    enc_gains,
    enc_inward,
    encoder_bias,
    enc_outward,
    enc_grow,
    enc_shrink,
    cross_key_value_weight,
    dec_gains,
    dec_inward,
    decoder_bias,
    dec_outward,
    cross_query,
    cross_outward,
    dec_grow,
    dec_shrink,
    grad_memory,
    grad_output,
):
    parts, blocks = lax.axis_size("narrow"), lax.axis_size("wide")
    wide_at, narrow_at = lax.axis_index("wide"), lax.axis_index("narrow")
    row_length = segments.shape[1]
    rows_here = segments.shape[0] // parts
    count = rows_here * row_length
    width = tokens.shape[1]
    slab = width // blocks
    inner_local = cross_query.shape[1]
    head_local = inner_local // HD
    heads = head_local * parts
    hidden_local = enc_grow.shape[1]
    questions, answers = answer_ids.shape
    dec_count = questions * answers

    def own_rows(array, size):
        return lax.dynamic_slice_in_dim(array, narrow_at * size, size, 0)

    tokens_here = own_rows(tokens, count).astype(F32)
    grad_memory_here = own_rows(grad_memory, count).astype(F32)
    segments_here = own_rows(segments, rows_here)
    question_here = own_rows(question, rows_here)

    def slabs(*matrices):
        return jnp.concatenate([m.reshape(width, -1) for m in matrices], axis=1).reshape(blocks, slab, -1)

    def joined(whole):
        return whole.reshape(parts, width, -1)

    attn_all = joined(gather_weights(slabs(enc_inward, enc_outward.T)))
    ffn_all = joined(
        gather_weights(
            jnp.concatenate(
                [
                    enc_grow.reshape(blocks, slab, hidden_local),
                    enc_shrink.reshape(blocks, -1, width),
                ],
                axis=-1,
            )
            if hidden_local == width
            else slabs(enc_grow, enc_shrink.T)
        )
    )
    cross_all = joined(gather_weights(slabs(cross_key_value_weight, cross_outward.T)))
    in_all, out_all = attn_all[:, :, : 3 * inner_local], attn_all[:, :, 3 * inner_local :]
    grow_all = ffn_all[:, :, :hidden_local]
    shrink_all = ffn_all[:, :, hidden_local:]
    kv_all, cross_out_all = cross_all[:, :, : 2 * inner_local], cross_all[:, :, 2 * inner_local :]

    table_all = spread_rows(encoder_bias.T)
    indicator = bucket_lookup(bucket_both(row_length), encoder_bias.shape[0])
    bias_all = jnp.einsum("uxe,cu->cxe", indicator, table_all, precision=FULL)
    allowed = (segments_here[:, :, None] == segments_here[:, None, :])[:, None]
    first_values, first_inv = norm_rows(tokens_here, enc_gains[0])
    first_normed = first_values.astype(BF16)

    def heads_of(projected, kinds):
        split = projected.reshape(rows_here, row_length, parts, kinds, head_local, HD)
        return [split[:, :, :, kind].reshape(rows_here, row_length, heads, HD) for kind in range(kinds)]

    projected = dot("td,zdf->tzf", first_normed, in_all).astype(BF16)
    queries, keys, values = heads_of(projected, 3)
    context, logsum = softmax_forward(queries, keys, values, bias_all, allowed)
    context_flat = context.reshape(count, parts, inner_local)
    hidden = tokens_here + dot("tzi,zdi->td", context_flat, out_all)
    second_values, second_inv = norm_rows(hidden, enc_gains[1])
    second_normed = second_values.astype(BF16)
    enc_grown = dot("td,zdf->tzf", second_normed, grow_all)
    enc_act = smooth_gate(enc_grown).astype(BF16)
    enc_summed = hidden + dot("tzf,zfd->td", enc_act, shrink_all)
    final_values, final_inv = norm_rows(enc_summed, enc_gains[2])
    memory = final_values.astype(BF16)
    kv = dot("td,zdf->tzf", memory, kv_all).astype(BF16)
    kv_split = kv.reshape(count, parts, 2, head_local, HD)
    cross_keys = kv_split[:, :, 0].reshape(count, heads, HD)
    cross_values = kv_split[:, :, 1].reshape(count, heads, HD)

    vocab_local = vocab_table.shape[0]
    vocab_ids = wide_at * vocab_local + jnp.arange(vocab_local, dtype=jnp.int32)
    one_hot = (answer_ids.reshape(-1)[:, None] == vocab_ids[None, :]).astype(BF16)
    embedded = exchange_sum(dot("qv,vd->qd", one_hot, vocab_table), "wide")
    dec_indicator = bucket_lookup(causal_bucket_ids(answers), decoder_bias.shape[0])
    dec_bias = jnp.einsum("uxe,uc->cxe", dec_indicator, decoder_bias, precision=FULL)
    places = jnp.arange(answers, dtype=jnp.int32)
    dec_allowed = (places[:, None] >= places[None, :])[None, None]
    zero_values, zero_inv = norm_rows(embedded, dec_gains[0])
    dec_normed = zero_values.astype(BF16)
    dec_projected = dot("td,dpf->ptf", dec_normed, dec_inward).astype(BF16)
    dec_queries, dec_keys, dec_values = [
        dec_projected[kind].reshape(questions, answers, head_local, HD) for kind in range(3)
    ]
    dec_context, dec_logsum = softmax_forward(dec_queries, dec_keys, dec_values, dec_bias, dec_allowed)
    dec_context = dec_context.reshape(dec_count, inner_local)
    dec_first = embedded + exchange_sum(dot("ti,id->td", dec_context, dec_outward), "narrow")
    cross_values_f, cross_inv = norm_rows(dec_first, dec_gains[1])
    cross_normed = cross_values_f.astype(BF16)
    cross_queries = dot("td,di->ti", cross_normed, cross_query).astype(BF16)
    queries_all = spread_rows(cross_queries[None])
    query_heads = queries_all.reshape(parts, dec_count, head_local, HD).transpose(1, 0, 2, 3)
    query_heads = query_heads.reshape(dec_count, heads, HD)

    token_question = jnp.repeat(question_here, row_length)
    dec_question = jnp.arange(dec_count, dtype=jnp.int32) // answers
    cross_allowed = (dec_question[:, None] == token_question[None, :])[None]
    cross_scores = dot("qhe,the->hqt", query_heads, cross_keys)
    cross_masked = jnp.where(cross_allowed, cross_scores, MASKED)
    local_max = jnp.max(cross_masked, axis=-1)
    exponent = jnp.where(cross_allowed, jnp.exp(cross_masked - local_max[:, :, None]), 0.0)
    high = exponent.astype(BF16)
    low = (exponent - high.astype(F32)).astype(BF16)
    local_sums = dot("hqt,the->hqe", high, cross_values) + dot("hqt,the->hqe", low, cross_values)
    stats = (local_max, jnp.sum(exponent, axis=-1), local_sums)
    for axis in ("wide", "narrow"):
        for bit in bits_of(lax.axis_size(axis)):
            stats = merge_stats(stats, swap(stats, axis, bit))
    whole_max, whole_total, whole_sums = stats
    cross_logsum = whole_max + jnp.log(whole_total)
    cross_exact = (whole_sums / whole_total[:, :, None]).transpose(1, 0, 2)
    cross_context = cross_exact.reshape(dec_count, -1).astype(BF16)
    cross_probs = jnp.where(cross_allowed, jnp.exp(cross_masked - cross_logsum[:, :, None]), 0.0)
    cross_weights = cross_probs.astype(BF16)

    dec_second = dec_first + dot("tzi,zdi->td", cross_context.reshape(dec_count, parts, -1), cross_out_all)
    third_values, third_inv = norm_rows(dec_second, dec_gains[2])
    third_normed = third_values.astype(BF16)
    dec_grown = dot("td,df->tf", third_normed, dec_grow)
    dec_act = smooth_gate(dec_grown).astype(BF16)
    grad_out = grad_output.astype(F32)
    grad_dec_grown = smooth_gate_back(dec_grown, dot("nd,fd->nf", grad_output, dec_shrink)).astype(BF16)
    third_part, output_part = exchange_sum(
        (dot("nf,df->nd", grad_dec_grown, dec_grow), dot("tf,fd->td", dec_act, dec_shrink)), "narrow"
    )
    output = (dec_second + output_part).astype(BF16)
    grad_dec_shrink = dot("nf,nd->fd", dec_act, grad_output)
    grad_dec_grow = dot("nd,nf->df", third_normed, grad_dec_grown)
    grad_third, third_gain = norm_back(third_part, dec_second, third_inv, dec_gains[2])
    grad_dec_second = grad_out + grad_third
    grad_cbranch = grad_dec_second.astype(BF16)
    grad_cross_context = dot("td,zdi->tzi", grad_cbranch, cross_out_all).astype(BF16)
    grad_cheads = grad_cross_context.reshape(dec_count, heads, HD)
    context_local = lax.dynamic_slice_in_dim(cross_context, narrow_at * inner_local, inner_local, 1)
    grad_cross_outward = dot("qi,qd->id", context_local, grad_cbranch)
    cross_delta = jnp.einsum("qhe,qhe->hq", grad_cheads.astype(F32), cross_exact, precision=FULL)
    grad_cprobs = dot("qhe,the->hqt", grad_cheads, cross_values)
    grad_cross_scores = (cross_probs * (grad_cprobs - cross_delta[:, :, None])).astype(BF16)
    grad_kv_values = dot("hqt,qhe->the", cross_weights, grad_cheads)
    grad_kv_keys = dot("hqt,qhe->the", grad_cross_scores, query_heads)
    query_part = dot("hqt,the->qhe", grad_cross_scores, cross_keys).reshape(dec_count, -1)
    grad_kv = jnp.stack(
        [g.reshape(count, parts, inner_local) for g in (grad_kv_keys, grad_kv_values)], axis=2
    ).astype(BF16)
    grad_kv = grad_kv.reshape(count, parts, 2 * inner_local)

    def scattered(whole):
        return scatter_sums(whole.astype(BF16).reshape(parts, blocks, slab, -1))

    memory_part = dot("tzf,zdf->td", grad_kv, kv_all)
    sent_cross = scattered(dot("td,tzf->zdf", memory, grad_kv))
    grad_final = memory_part + grad_memory_here
    grad_enc_summed, final_gain = norm_back(grad_final, enc_summed, final_inv, enc_gains[2])
    grad_branch_ffn = grad_enc_summed.astype(BF16)
    grad_enc_act = dot("td,zfd->tzf", grad_branch_ffn, shrink_all)
    grad_enc_grown = smooth_gate_back(enc_grown, grad_enc_act).astype(BF16)
    sent_ffn = scattered(
        jnp.concatenate(
            [
                dot("td,tzf->zdf", second_normed, grad_enc_grown),
                dot("td,tzf->zdf", grad_branch_ffn, enc_act),
            ],
            axis=-1,
        )
    )
    second_part = dot("tzf,zdf->td", grad_enc_grown, grow_all)
    grad_second_norm, second_gain = norm_back(second_part, hidden, second_inv, enc_gains[1])
    grad_enc_hidden = grad_enc_summed + grad_second_norm
    grad_branch_attn = grad_enc_hidden.astype(BF16)
    grad_context = dot("td,zdi->tzi", grad_branch_attn, out_all).astype(BF16)
    grad_heads = grad_context.reshape(rows_here, row_length, heads, HD)
    grad_qkv, bias_rows = softmax_backward(
        queries, keys, values, bias_all, allowed, logsum, grad_heads
    )
    grad_projected = jnp.stack([g.reshape(count, parts, inner_local) for g in grad_qkv], axis=2)
    grad_projected = grad_projected.reshape(count, parts, 3 * inner_local)
    sent_attn = scattered(
        jnp.concatenate(
            [
                dot("td,tzf->zdf", first_normed, grad_projected),
                dot("td,tzf->zdf", grad_branch_attn, context_flat),
            ],
            axis=-1,
        )
    )
    first_part = dot("tzf,zdf->td", grad_projected, in_all)
    grad_first_norm, first_gain = norm_back(first_part, tokens_here, first_inv, enc_gains[0])
    grad_tokens = spread_rows((grad_enc_hidden + grad_first_norm).astype(BF16))
    memory_out = spread_rows(memory)

    enc_gain_terms = jnp.stack([jnp.sum(g, axis=0) for g in (first_gain, second_gain, final_gain)])
    enc_bias_local = jnp.einsum("jia,xia->xj", bias_rows, indicator, precision=FULL)
    enc_gain_sums, enc_bias_sums = exchange_sum(
        exchange_sum((enc_gain_terms, enc_bias_local), "wide"), "narrow"
    )
    grad_enc_bias = lax.dynamic_slice_in_dim(enc_bias_sums, narrow_at * head_local, head_local, 1)

    grad_cross_queries_all = exchange_sum(exchange_sum(query_part, "wide"), "narrow").astype(BF16)
    grad_cross_queries = lax.dynamic_slice_in_dim(
        grad_cross_queries_all, narrow_at * inner_local, inner_local, 1
    )
    grad_cross_query = dot("qd,qi->di", cross_normed, grad_cross_queries)
    cross_part = exchange_sum(dot("qi,di->qd", grad_cross_queries, cross_query), "narrow")
    grad_cross_norm, cross_gain = norm_back(cross_part, dec_first, cross_inv, dec_gains[1])
    grad_dec_first = grad_dec_second + grad_cross_norm
    grad_sbranch = grad_dec_first.astype(BF16)
    grad_dec_outward = dot("ti,td->id", dec_context, grad_sbranch)
    grad_dec_heads = dot("td,id->ti", grad_sbranch, dec_outward).astype(BF16)
    grad_dec_qkv, dec_bias_rows = softmax_backward(
        dec_queries,
        dec_keys,
        dec_values,
        dec_bias,
        dec_allowed,
        dec_logsum,
        grad_dec_heads.reshape(questions, answers, head_local, HD),
    )
    grad_dec_projected = jnp.stack([g.reshape(dec_count, inner_local) for g in grad_dec_qkv])
    grad_dec_inward = dot("td,ptf->dpf", dec_normed, grad_dec_projected)
    zero_part = exchange_sum(dot("ptf,dpf->td", grad_dec_projected, dec_inward), "narrow")
    grad_zero, zero_gain = norm_back(zero_part, embedded, zero_inv, dec_gains[0])
    grad_embedded = grad_dec_first + grad_zero
    grad_vocab_table = jnp.einsum("qv,qd->vd", one_hot.astype(F32), grad_embedded, precision=FULL)
    gradient_decoder_bias = jnp.einsum("jia,xia->xj", dec_bias_rows, dec_indicator, precision=FULL)
    grad_dec_gains = jnp.stack([jnp.sum(g, axis=0) for g in (zero_gain, cross_gain, third_gain)])

    sent_inward = sent_attn[:, : 3 * inner_local].reshape(slab, 3, inner_local)
    sent_outward = sent_attn[:, 3 * inner_local :].T
    sent_grow = sent_ffn[:, :hidden_local]
    sent_shrink = sent_ffn[:, hidden_local:].T
    return (
        memory_out,
        output,
        grad_tokens,
        grad_vocab_table,
        enc_gain_sums,
        sent_inward,
        grad_enc_bias,
        sent_outward,
        sent_grow,
        sent_shrink,
        sent_cross.reshape(slab, 2, inner_local),
        grad_dec_gains,
        grad_dec_inward,
        gradient_decoder_bias,
        grad_dec_outward,
        grad_cross_query,
        grad_cross_outward,
        grad_dec_grow,
        grad_dec_shrink,
    )


def solution(mesh):
    in_specs = (
        P("wide", None),
        P("wide", None),
        P("wide"),
        P(),
        P("wide", None),
        P(),
        P(None, None, "narrow"),
        P(None, "narrow"),
        P("narrow", None),
        P(None, "narrow"),
        P("narrow", None),
        P(None, None, "narrow"),
        P(),
        P(None, None, "narrow"),
        P(None, "narrow"),
        P("narrow", None),
        P(None, "narrow"),
        P("narrow", None),
        P(None, "narrow"),
        P("narrow", None),
        P("wide", None),
        P(),
    )
    out_specs = (
        P("wide", None),
        P(),
        P("wide", None),
        P("wide", None),
        P(),
        P("wide", None, "narrow"),
        P(None, "narrow"),
        P("narrow", "wide"),
        P("wide", "narrow"),
        P("narrow", "wide"),
        P("wide", None, "narrow"),
        P(),
        P(None, None, "narrow"),
        P(None, "narrow"),
        P("narrow", None),
        P(None, "narrow"),
        P("narrow", None),
        P(None, "narrow"),
        P("narrow", None),
    )
    return jax.shard_map(
        per_device, mesh=mesh, in_specs=in_specs, out_specs=out_specs, check_vma=False
    )
```

```python
import functools
import jax
import jax.numpy as jnp
import numpy as np
from jax import lax
from jax.experimental import pallas as pl
from jax.experimental.pallas import tpu as pltpu
from jax.sharding import PartitionSpec as P

HD = 64
SLABS = 8
EPSILON = 1e-06
BOTH_EDGES = (12, 16, 23, 32, 46, 64, 91)
CAUSAL_EDGES = (19, 21, 24, 27, 31, 35, 40, 46, 52, 59, 67, 77, 87, 99, 113)
FULL = lax.Precision.HIGHEST
F32 = jnp.float32
BF16 = jnp.bfloat16
I32 = jnp.int32
MASKED = -1e30
MIB = 1 << 20


def bits_of(count):
    return [1 << k for k in range(count.bit_length() - 1)]


def swap(value, axis, bit):
    count = lax.axis_size(axis)
    return lax.ppermute(value, axis, [(i, i ^ bit) for i in range(count)])


def exchange_sum(value, axis):
    for bit in bits_of(lax.axis_size(axis)):
        value = value + swap(value, axis, bit)
    return value


def exchange_pair(value, axis):
    bits = bits_of(lax.axis_size(axis))
    for bit in bits[:-1]:
        value = value + swap(value, axis, bit)
    return value, swap(value, axis, bits[-1])


def rounded_sum(*parts):
    return sum(part.astype(F32) for part in parts).astype(BF16)


def spread_rows(mine):
    parts = lax.axis_size("narrow")
    narrow_at = lax.axis_index("narrow")
    whole = jnp.zeros((parts,) + mine.shape, mine.dtype)
    for offset in range(parts):
        piece = mine if offset == 0 else swap(mine, "narrow", offset)
        whole = lax.dynamic_update_index_in_dim(whole, piece, narrow_at ^ offset, 0)
    return whole.reshape((-1,) + mine.shape[1:])


def slab_bits():
    low = lax.axis_size("wide") // SLABS
    return [low * bit for bit in bits_of(SLABS)], lax.axis_index("wide") // low


def gather_pieces(mine):
    parts = lax.axis_size("narrow")
    (low, a, b), _ = slab_bits()
    others = jnp.stack([swap(mine, "narrow", offset) for offset in range(1, parts)])
    half = mine.shape[0] // 2
    over_a, over_b = swap(others, "wide", a), swap(others, "wide", b)
    far_a = swap(over_b[:, :half], "wide", a)
    far_b = swap(over_a[:, half:], "wide", b)
    pieces = [(0, 0, others), (2, 0, over_a), (4, 0, over_b), (6, 0, far_a), (6, half, far_b)]
    return pieces + [(at ^ 1, first, swap(piece, "wide", low)) for at, first, piece in pieces]


def scatter_sums(far, rest, keep):
    (low, a, b), _ = slab_bits()
    got_far, got = swap(far, "wide", low), swap(rest, "wide", low)
    half = far.shape[0] // 2
    from_a = swap(rounded_sum(keep[3, :half], got_far[:half]), "wide", a)
    from_b = swap(rounded_sum(keep[3, half:], got_far[half:]), "wide", b)
    send_b = jnp.concatenate(
        [rounded_sum(keep[2, :half], got[2, :half], from_a), rounded_sum(keep[2, half:], got[2, half:])]
    )
    send_a = jnp.concatenate(
        [rounded_sum(keep[1, :half], got[1, :half]), rounded_sum(keep[1, half:], got[1, half:], from_b)]
    )
    got_a, got_b = swap(send_a, "wide", a), swap(send_b, "wide", b)
    result = sum(part.astype(F32) for part in (keep[0, 0], got[0, 0], got_a[0], got_b[0]))
    for offset in range(1, far.shape[0]):
        term = rounded_sum(keep[0, offset], got[0, offset], got_a[offset], got_b[offset])
        result = result + swap(term, "narrow", offset).astype(F32)
    wide_at, slab = lax.axis_index("wide"), result.shape[0]
    for bit in bits_of(low)[::-1]:
        result = result.reshape(2, -1, result.shape[-1])
        upper = (wide_at & bit) // bit
        held = lax.dynamic_index_in_dim(result, upper, 0, keepdims=False)
        sent = lax.dynamic_index_in_dim(result, 1 - upper, 0, keepdims=False)
        result = held + swap(sent, "wide", bit)
    return result


def mm(left, right):
    return lax.dot_general(left, right, (((1,), (0,)), ((), ())), preferred_element_type=F32)


def mm_t(left, right):
    return lax.dot_general(left, right, (((1,), (1,)), ((), ())), preferred_element_type=F32)


def t_mm(left, right):
    return lax.dot_general(left, right, (((0,), (0,)), ((), ())), preferred_element_type=F32)


def exact_mm(left, right):
    return lax.dot_general(
        left, right, (((1,), (0,)), ((), ())), precision=FULL, preferred_element_type=F32
    )


def norm(values, gain):
    inv = lax.rsqrt(jnp.mean(values * values, axis=-1, keepdims=True) + EPSILON)
    return values * inv * gain, inv


def norm_back(upstream, values, gain):
    inv = lax.rsqrt(jnp.mean(values * values, axis=-1, keepdims=True) + EPSILON)
    scaled = upstream * gain
    pull = jnp.mean(scaled * values, axis=-1, keepdims=True)
    return inv * scaled - values * (inv * inv * inv) * pull, jnp.sum(
        upstream * values * inv, axis=0, keepdims=True
    )


def gelu_both(x):
    scale = np.float32(np.sqrt(2.0 / np.pi))
    square = x * x
    bent = jnp.tanh(scale * (x + 0.044715 * square * x))
    half = 0.5 * (1.0 + bent)
    slope = half + 0.5 * x * (1.0 - bent * bent) * scale * (1.0 + 3 * 0.044715 * square)
    return x * half, slope


def toeplitz(row, rows):
    spread = jnp.broadcast_to(row, (rows, row.shape[1]))
    return pltpu.roll(spread, 0, 1, stride=1, stride_axis=0)


def diagonal_sums(matrix, lanes):
    rows, columns = matrix.shape
    flip = lax.broadcasted_iota(I32, (rows, rows), 0) + lax.broadcasted_iota(I32, (rows, rows), 1)
    turned = mm(jnp.where(flip == rows - 1, 1.0, 0.0).astype(BF16), matrix)
    if columns < lanes:
        turned = jnp.concatenate([turned, jnp.zeros((rows, lanes - columns), F32)], axis=1)
    turned = pltpu.roll(turned, 0, 1, stride=1, stride_axis=0)
    return jnp.sum(turned, axis=0, keepdims=True)


class In:
    def __init__(self, array, space=pltpu.VMEM):
        self.array = array
        self.spec = pl.BlockSpec(memory_space=space)


def smem(array):
    return In(array, pltpu.SMEM)


def anywhere(array):
    return In(array, pl.ANY)


def call(kernel, name, inputs, outs, scratch=(), vmem=24, us=2):
    inputs = [i if isinstance(i, In) else In(i) for i in inputs]
    return pl.pallas_call(
        kernel,
        out_shape=[jax.ShapeDtypeStruct(shape, dtype) for shape, dtype in outs],
        in_specs=[i.spec for i in inputs],
        out_specs=[pl.BlockSpec(memory_space=pltpu.VMEM)] * len(outs),
        scratch_shapes=list(scratch),
        compiler_params=pltpu.CompilerParams(vmem_limit_bytes=vmem * MIB),
        cost_estimate=pl.CostEstimate(flops=int(us * 1.1e9), bytes_accessed=0, transcendentals=0),
        name=name,
    )(*[i.array for i in inputs])


class Weights:
    def __init__(self, local, pieces, parts):
        self.local, self.pieces, self.parts = local, pieces, parts
        self.blocks = 1 + max(block for _, block, _ in local)
        self.rows = local[0][0].shape[1]
        self.slab = self.rows // SLABS
        self.inputs = [anywhere(array) for array, _, _ in local]
        self.inputs += [anywhere(piece) for _, _, piece in pieces]
        per_piece = sum(len(self.targets(first, piece.shape[1])) for _, first, piece in pieces)
        self.count = len(local) + (parts - 1) * per_piece
        self.scratch = [
            pltpu.VMEM((parts, self.blocks, self.rows, local[0][0].shape[1]), BF16),
            pltpu.SemaphoreType.DMA((self.count,)),
        ]

    def targets(self, first, rows):
        if rows < self.slab:
            return [(0, 0, first, rows)]
        return [
            (at, (first + at) // self.slab, 0, self.slab) for at in range(0, rows, self.slab)
        ]

    def start(self, where, refs, held, sem):
        slab, narrow_at = where[0], where[1]
        groups = [[] for _ in range(self.parts)]
        for (array, block, first), ref in zip(self.local, refs):
            groups[0].append((ref, held.at[narrow_at, block, pl.ds(first, array.shape[0])]))
        for offset in range(1, self.parts):
            for (at, first, piece), ref in zip(self.pieces, refs[len(self.local) :]):
                for source, block, row, rows in self.targets(first, piece.shape[1]):
                    target = pl.multiple_of((slab ^ at) * self.slab + row, 16)
                    groups[offset].append(
                        (
                            ref.at[offset - 1, pl.ds(source, rows)],
                            held.at[narrow_at ^ offset, block, pl.ds(target, rows)],
                        )
                    )
        made, number = [], 0
        for group in groups:
            copies = []
            for source, target in group:
                copies.append(pltpu.make_async_copy(source, target, sem.at[number]))
                copies[-1].start()
                number += 1
            made.append(copies)
        return made


def fetch_rows(weights, first, held, sem):
    copy = pltpu.make_async_copy(weights.at[:, 0, pl.ds(first, held.shape[1])], held, sem)
    copy.start()
    return copy


def wait_all(copies):
    for copy in copies:
        copy.wait()


def embed_rows(where, ids, table):
    count, (rows, width) = ids.shape[0], table.shape

    def kernel(where_ref, ids_ref, table_ref, out_ref, tiles, sums, sem):
        base = where_ref[3] * rows

        def tile_of(i):
            local = jnp.clip(ids_ref[i] - base, 0, rows - 1)
            return pl.multiple_of((local >> 4) << 4, 16)

        def copy(i):
            return pltpu.make_async_copy(
                table_ref.at[pl.ds(tile_of(i), 16)], tiles.at[i], sem.at[i]
            )

        @pl.loop(0, count)
        def _(i):
            copy(i).start()

        @pl.loop(0, count)
        def _(i):
            copy(i).wait()
            local = ids_ref[i] - base
            wanted = jnp.where((local >= 0) & (local < rows), local & 15, 16)
            match = lax.broadcasted_iota(I32, (16, width), 0) == wanted
            row = jnp.sum(jnp.where(match, tiles[i].astype(F32), 0.0), axis=0, keepdims=True)
            sums[pl.ds(i, 1), :] = row

        out_ref[...] = sums[...].astype(BF16)

    return call(
        kernel,
        "embed_rows",
        [smem(where), smem(ids), anywhere(table)],
        [((count, width), BF16)],
        [pltpu.VMEM((count, 16, width), BF16), pltpu.VMEM((count, width), F32), pltpu.SemaphoreType.DMA((count,))],
    )[0]


def causal_mask(count, answers):
    query = lax.broadcasted_iota(I32, (count, count), 0)
    key = lax.broadcasted_iota(I32, (count, count), 1)
    return (query // answers == key // answers) & (key <= query)


def masked_softmax(scores, allowed):
    masked = jnp.where(allowed, scores, MASKED)
    exponent = jnp.exp(masked - jnp.max(masked, axis=-1, keepdims=True))
    return exponent / jnp.sum(exponent, axis=-1, keepdims=True)


def decoder_self(embedded, gains, inward, outward, bias_line, answers):
    count, width = embedded.shape
    inner = outward.shape[0]

    def kernel(x_ref, gains_ref, in_ref, out_w_ref, line_ref, normed_ref, proj_ref, ctx_ref, part_ref):
        x = x_ref[...].astype(F32)
        normed = norm(x, gains_ref[0:1])[0].astype(BF16)
        normed_ref[...] = normed
        proj = mm_t(normed, in_ref[...]).astype(BF16)
        proj_ref[...] = proj
        allowed = causal_mask(count, answers)
        contexts = []
        for h in range(inner // HD):
            q, k, v = [proj[:, s * inner + h * HD : s * inner + (h + 1) * HD] for s in range(3)]
            scores = mm_t(q, k) + toeplitz(line_ref[h : h + 1], count)[:, :count]
            contexts.append(mm(masked_softmax(scores, allowed).astype(BF16), v).astype(BF16))
        context = jnp.concatenate(contexts, axis=1)
        ctx_ref[...] = context
        part_ref[...] = mm(context, out_w_ref[...])

    return call(
        kernel,
        "decoder_self",
        [embedded, gains, inward, outward, bias_line],
        [((count, width), BF16), ((count, 3 * inner), BF16), ((count, inner), BF16), ((count, width), F32)],
    )


def encoder_attention(where, tokens, segments, gains, bias_line, weights):
    length, width = segments.shape[1], tokens.shape[1]
    inner = bias_line.shape[1] * HD
    parts = weights.parts

    def kernel(where_ref, tokens_ref, seg_ref, gains_ref, line_ref, *refs):
        pieces, refs = refs[: len(weights.inputs)], refs[len(weights.inputs) :]
        hidden_ref, normed_ref, qkv_ref, ctx_ref, held, sem, own, own_sem = refs
        narrow_at = where_ref[1]
        fetch = pltpu.make_async_copy(
            tokens_ref.at[pl.ds(pl.multiple_of(narrow_at * length, 16), length)], own, own_sem
        )
        fetch.start()
        loads = weights.start(where_ref, pieces, held, sem)
        allowed = same_segment(seg_ref[pl.ds(narrow_at, 1), :])
        fetch.wait()
        x = own[...].astype(F32)
        normed = norm(x, gains_ref[0:1])[0].astype(BF16)
        normed_ref[...] = normed
        hidden_ref[...] = x
        for copies in loads:
            wait_all(copies)

        @pl.loop(0, parts)
        def _(z):
            proj = mm_t(normed, held[z, 0, : 3 * inner]).astype(BF16)
            qkv_ref[z] = proj
            contexts = []
            for h in range(inner // HD):
                q, k, v = [proj[:, s * inner + h * HD : s * inner + (h + 1) * HD] for s in range(3)]
                line = line_ref[z ^ narrow_at, h : h + 1]
                scores = mm_t(q, k) + toeplitz(line, length)[:, :length]
                contexts.append(mm(masked_softmax(scores, allowed).astype(BF16), v).astype(BF16))
            context = jnp.concatenate(contexts, axis=1)
            ctx_ref[z] = context
            hidden_ref[...] += mm(context, held[z, 0, 3 * inner :])

    return call(
        kernel,
        "encoder_attention",
        [smem(where), anywhere(tokens), segments, gains, bias_line] + weights.inputs,
        [
            ((length, width), F32),
            ((length, width), BF16),
            ((parts, length, 3 * inner), BF16),
            ((parts, length, inner), BF16),
        ],
        weights.scratch + [pltpu.VMEM((length, width), BF16), pltpu.SemaphoreType.DMA],
        vmem=32,
        us=15,
    )


def same_segment(row):
    length = row.shape[1]
    across = jnp.broadcast_to(row.astype(F32), (length, length))
    diagonal = lax.broadcasted_iota(I32, (length, length), 0) == lax.broadcasted_iota(
        I32, (length, length), 1
    )
    down = jnp.sum(jnp.where(diagonal, across, 0.0), axis=1, keepdims=True)
    return across == down


def encoder_ffn(where, hidden, gains, weights):
    length, width = hidden.shape
    parts = weights.parts
    units = weights.rows

    def kernel(where_ref, hidden_ref, gains_ref, *refs):
        pieces, refs = refs[: len(weights.inputs)], refs[len(weights.inputs) :]
        normed_ref, act_ref, slope_ref, summed_ref, memory_ref, held, sem = refs
        loads = weights.start(where_ref, pieces, held, sem)
        narrow_at = where_ref[1]
        x = hidden_ref[...]
        normed = norm(x, gains_ref[1:2])[0].astype(BF16)
        normed_ref[...] = normed
        total = x
        for offset in range(parts):
            z = narrow_at ^ offset
            wait_all(loads[offset])
            act, slope = gelu_both(mm(normed, held[z, 1]))
            act = act.astype(BF16)
            act_ref[z] = act
            slope_ref[z] = slope
            total = total + mm(act, held[z, 0])
        summed_ref[...] = total
        memory_ref[...] = norm(total, gains_ref[2:3])[0].astype(BF16)

    return call(
        kernel,
        "encoder_ffn",
        [smem(where), hidden, gains] + weights.inputs,
        [
            ((length, width), BF16),
            ((parts, length, units), BF16),
            ((parts, length, units), F32),
            ((length, width), F32),
            ((length, width), BF16),
        ],
        weights.scratch,
        vmem=40,
        us=17,
    )


def cross_forward(where, memory, embedded, self_sums, gains, weights, answers, inner):
    length, width = memory.shape
    count = embedded.shape[0]
    parts = weights.parts
    heads = inner // HD

    def kernel(where_ref, memory_ref, embedded_ref, one_ref, two_ref, gains_ref, *refs):
        pieces, refs = refs[: len(weights.inputs)], refs[len(weights.inputs) :]
        first_ref, normed_ref, q_ref, kv_ref, stats_ref, held, sem = refs
        loads = weights.start(where_ref, pieces, held, sem)
        narrow_at = where_ref[1]
        first = embedded_ref[...].astype(F32) + (one_ref[...] + two_ref[...])
        first_ref[...] = first
        normed = norm(first, gains_ref[1:2])[0].astype(BF16)
        normed_ref[...] = normed
        memory = memory_ref[...]
        mine = lax.broadcasted_iota(I32, (count, 1), 0) // answers == where_ref[2]
        lane = lax.broadcasted_iota(I32, (count, 128), 1)
        stats = jnp.where(lane < 64, MASKED, 0.0)
        for copies in loads:
            wait_all(copies)
        sums = []
        for z in range(parts):
            kv = mm_t(memory, held[z, 0, : 2 * inner]).astype(BF16)
            kv_ref[z] = kv
            queries = mm_t(normed, held[z, 0, 3 * inner :]).astype(BF16)
            q_ref[z] = queries
            for h in range(heads):
                k, v = [kv[:, s * inner + h * HD : s * inner + (h + 1) * HD] for s in range(2)]
                scores = mm_t(queries[:, h * HD : (h + 1) * HD], k)
                largest = jnp.max(scores, axis=-1, keepdims=True)
                exponent = jnp.where(mine, jnp.exp(scores - largest), 0.0)
                high = exponent.astype(BF16)
                low = (exponent - high.astype(F32)).astype(BF16)
                sums.append(mm(high, v) + mm(low, v))
                at = z * heads + h
                stats = jnp.where(lane == at, jnp.where(mine, largest, MASKED), stats)
                stats = jnp.where(lane == 64 + at, jnp.sum(exponent, axis=-1, keepdims=True), stats)
        stats_ref[...] = jnp.concatenate(sums + [stats], axis=1)

    return call(
        kernel,
        "cross_forward",
        [smem(where), memory, embedded, *self_sums, gains] + weights.inputs,
        [
            ((count, width), F32),
            ((count, width), BF16),
            ((parts, count, inner), BF16),
            ((parts, length, 2 * inner), BF16),
            ((count, width + 128), F32),
            (weights.scratch[0].shape, BF16),
        ],
        weights.scratch[1:],
        vmem=32,
        us=9,
    )


def spread_heads(stats, first, heads):
    count = stats.shape[0]
    return jnp.concatenate(
        [jnp.broadcast_to(stats[:, first + h : first + h + 1], (count, HD)) for h in range(heads)], axis=1
    )


def merge(one, two):
    width = one.shape[1] - 128
    heads = width // HD
    stats_one, stats_two = one[:, width:], two[:, width:]

    def join(largest_one, largest_two, value_one, value_two):
        ahead = largest_one >= largest_two
        scale = jnp.exp(
            jnp.where(ahead, largest_two, largest_one) - jnp.where(ahead, largest_one, largest_two)
        )
        return jnp.where(ahead, value_one, value_two) + scale * jnp.where(ahead, value_two, value_one)

    sums = join(
        spread_heads(stats_one, 0, heads), spread_heads(stats_two, 0, heads), one[:, :width], two[:, :width]
    )
    totals = join(stats_one[:, :64], stats_two[:, :64], stats_one[:, 64:], stats_two[:, 64:])
    stats = jnp.concatenate([jnp.maximum(stats_one[:, :64], stats_two[:, :64]), totals], axis=1)
    return sums, stats


def merge_stats(one, two):
    def kernel(one_ref, two_ref, out_ref):
        sums, stats = merge(one_ref[...], two_ref[...])
        out_ref[...] = jnp.concatenate([sums, stats], axis=1)

    return call(kernel, "merge_stats", [one, two], [(one.shape, F32)])[0]


def decoder_middle(one, two, first, cross_weights, gains, grow, shrink, grad_output, inner):
    count, width = first.shape
    parts = width // inner
    heads = width // HD

    def kernel(one_ref, two_ref, first_ref, out_w_ref, gains_ref, grow_ref, shrink_ref, up_ref, *refs):
        exact_ref, stats_ref, ctx_ref, second_ref, normed_ref, act_ref, back_ref, part_ref, out_ref, held, sem = refs
        fetch = fetch_rows(out_w_ref, 2 * inner, held, sem)
        sums, stats = merge(one_ref[...], two_ref[...])
        stats_ref[...] = stats
        exact = sums / spread_heads(stats, 64, heads)
        exact_ref[...] = exact
        context = exact.astype(BF16)
        ctx_ref[...] = context
        fetch.wait()
        branch = mm(context[:, :inner], held[0])
        for z in range(1, parts):
            branch = branch + mm(context[:, z * inner : (z + 1) * inner], held[z])
        second = first_ref[...] + branch
        second_ref[...] = second
        normed = norm(second, gains_ref[2:3])[0].astype(BF16)
        normed_ref[...] = normed
        act, slope = gelu_both(mm(normed, grow_ref[...]))
        act = act.astype(BF16)
        act_ref[...] = act
        back = (mm_t(up_ref[...], shrink_ref[...]) * slope).astype(BF16)
        back_ref[...] = back
        part_ref[...] = mm_t(back, grow_ref[...])
        out_ref[...] = mm(act, shrink_ref[...])

    units = grow.shape[1]
    return call(
        kernel,
        "decoder_middle",
        [
            one,
            two,
            first,
            anywhere(cross_weights),
            gains,
            grow,
            shrink,
            grad_output,
        ],
        [
            ((count, width), F32),
            ((count, 128), F32),
            ((count, width), BF16),
            ((count, width), F32),
            ((count, width), BF16),
            ((count, units), BF16),
            ((count, units), BF16),
            ((count, width), F32),
            ((count, width), F32),
        ],
        [pltpu.VMEM((parts, inner, width), BF16), pltpu.SemaphoreType.DMA],
    )


def cross_backward(
    where, third_sums, second, gains, grad_output, cross_weights, kv, queries, stats, exact,
    grad_memory, summed, enc_gains, answers,
):
    count, width = second.shape
    parts, length, inner = kv.shape[0], kv.shape[1], kv.shape[2] // 2
    heads = inner // HD

    def kernel(where_ref, one_ref, two_ref, second_ref, gains_ref, up_ref, weights_ref, kv_ref, q_ref, *refs):
        stats_ref, exact_ref, memory_ref, summed_ref, enc_gains_ref = refs[:5]
        grad_second_ref, branch_ref, grad_kv_ref, query_ref, grad_ref, low_ref, gain_ref, own, sem = refs[5:14]
        kv_held, kv_sem, out_held, out_sem = refs[14:]
        out_fetch = fetch_rows(weights_ref, 2 * inner, out_held, out_sem)
        kv_fetch = fetch_rows(weights_ref, 0, kv_held, kv_sem)
        fetch = pltpu.make_async_copy(
            memory_ref.at[pl.ds(pl.multiple_of(where_ref[1] * length, 16), length)], own, sem
        )
        fetch.start()
        grad_third, third_gain = norm_back(one_ref[...] + two_ref[...], second_ref[...], gains_ref[2:3])
        grad_second = up_ref[...].astype(F32) + grad_third
        grad_second_ref[...] = grad_second
        branch = grad_second.astype(BF16)
        branch_ref[...] = branch
        mine = lax.broadcasted_iota(I32, (count, 1), 0) // answers == where_ref[2]
        stats = stats_ref[...]
        logsum = stats[:, :64] + jnp.log(stats[:, 64:])
        exact = exact_ref[...]
        fetch.wait()
        total = own[...].astype(F32)
        out_fetch.wait()
        kv_fetch.wait()
        query_parts = []
        for z in range(parts):
            context = mm_t(branch, out_held[z]).astype(BF16)
            deltas = context.astype(F32) * exact[:, z * inner : (z + 1) * inner]
            grad_keys, grad_values = [], []
            for h in range(heads):
                at = z * heads + h
                k, v = [kv_ref[z, :, s * inner + h * HD : s * inner + (h + 1) * HD] for s in range(2)]
                q = q_ref[z, :, h * HD : (h + 1) * HD]
                up = context[:, h * HD : (h + 1) * HD]
                probs = jnp.where(mine, jnp.exp(mm_t(q, k) - logsum[:, at : at + 1]), 0.0)
                delta = jnp.sum(deltas[:, h * HD : (h + 1) * HD], axis=-1, keepdims=True)
                grad_scores = (probs * (mm_t(up, v) - delta)).astype(BF16)
                query_parts.append(mm(grad_scores, k))
                grad_keys.append(t_mm(grad_scores, q).astype(BF16))
                grad_values.append(t_mm(probs.astype(BF16), up).astype(BF16))
            grad_kv = jnp.concatenate(grad_keys + grad_values, axis=1)
            grad_kv_ref[z] = grad_kv
            total = total + mm(grad_kv, kv_held[z])
        query_ref[...] = jnp.concatenate(query_parts, axis=1)
        grad, gain = norm_back(total, summed_ref[...], enc_gains_ref[2:3])
        grad_ref[...] = grad
        low_ref[...] = grad.astype(BF16)
        gain_ref[...] = jnp.concatenate([gain, third_gain], axis=0)

    return call(
        kernel,
        "cross_backward",
        [
            smem(where),
            *third_sums,
            second,
            gains,
            grad_output,
            anywhere(cross_weights),
            kv,
            queries,
            stats,
            exact,
            anywhere(grad_memory),
            summed,
            enc_gains,
        ],
        [
            ((count, width), F32),
            ((count, width), BF16),
            (kv.shape, BF16),
            ((count, width), F32),
            ((length, width), F32),
            ((length, width), BF16),
            ((2, width), F32),
        ],
        [
            pltpu.VMEM((length, width), BF16),
            pltpu.SemaphoreType.DMA,
            pltpu.VMEM((parts, 2 * inner, width), BF16),
            pltpu.SemaphoreType.DMA,
            pltpu.VMEM((parts, inner, width), BF16),
            pltpu.SemaphoreType.DMA,
        ],
        vmem=32,
        us=9,
    )


def ffn_backward(where, grad_summed, slope, hidden, gains, weights):
    length, width = hidden.shape
    parts = weights.parts

    def kernel(where_ref, grad_ref, slope_ref, hidden_ref, gains_ref, *refs):
        pieces, refs = refs[: len(weights.inputs)], refs[len(weights.inputs) :]
        grown_ref, out_ref, gain_ref, held, sem = refs
        loads = weights.start(where_ref, pieces, held, sem)
        narrow_at = where_ref[1]
        grad = grad_ref[...]
        branch = grad.astype(BF16)
        total = jnp.zeros((length, width), F32)
        for offset in range(parts):
            z = narrow_at ^ offset
            wait_all(loads[offset])
            grown = (mm_t(branch, held[z, 0]) * slope_ref[z]).astype(BF16)
            grown_ref[z] = grown
            total = total + mm_t(grown, held[z, 1])
        pulled, gain = norm_back(total, hidden_ref[...], gains_ref[1:2])
        out_ref[...] = grad + pulled
        gain_ref[...] = gain

    return call(
        kernel,
        "ffn_backward",
        [smem(where), grad_summed, slope, hidden, gains] + weights.inputs,
        [(slope.shape, BF16), ((length, width), F32), ((1, width), F32)],
        weights.scratch,
        vmem=40,
        us=17,
    )


def weight_grads(where, pairs, name):
    parts, (length, width) = pairs[0][1].shape[0], pairs[0][0].shape
    lanes = sum(right.shape[-1] for _, right in pairs)
    rows = width // SLABS
    lefts = []
    for left, _ in pairs:
        if not any(left is known for known in lefts):
            lefts.append(left)

    def kernel(where_ref, *refs):
        left_refs, refs = refs[: len(lefts)], refs[len(lefts) :]
        right_refs, refs = refs[: len(pairs)], refs[len(pairs) :]
        far_ref, rest_ref, keep_ref, held = refs
        slab, narrow_at = where_ref[0], where_ref[1]
        turned = [ref[...].T for ref in left_refs]
        for offset in range(parts):
            first = 0
            for (left, right), ref in zip(pairs, right_refs):
                which = [number for number, known in enumerate(lefts) if known is left][0]
                last = first + right.shape[-1]
                held[:, first:last] = mm(turned[which], ref[narrow_at ^ offset]).astype(BF16)
                first = last
            for at in range(SLABS):
                block = held[pl.ds(pl.multiple_of((slab ^ at) * rows, 16), rows), :]
                if at == 7:
                    far_ref[offset] = block
                elif at & 1:
                    rest_ref[at >> 1, offset] = block
                else:
                    keep_ref[at >> 1, offset] = block

    return call(
        kernel,
        name,
        [smem(where)] + lefts + [right for _, right in pairs],
        [
            ((parts, rows, lanes), BF16),
            ((3, parts, rows, lanes), BF16),
            ((4, parts, rows, lanes), BF16),
        ],
        [pltpu.VMEM((width, lanes), BF16)],
        vmem=40,
        us=6,
    )


def attention_backward(
    where, grad_hidden, hidden_gains, normed, qkv, tokens, segments, gains, bias_line, buckets, weights
):
    length, width = grad_hidden.shape
    inner = bias_line.shape[1] * HD
    heads = inner // HD
    parts = weights.parts
    lanes, bucket_count = buckets.shape

    def kernel(where_ref, grad_ref, known_ref, second_ref, qkv_ref, tokens_ref, seg_ref, gains_ref, line_ref, buckets_ref, *refs):
        pieces, refs = refs[: len(weights.inputs)], refs[len(weights.inputs) :]
        branch_ref, dqkv_ref, out_ref, shared_ref, held, sem, own, own_sem, sums, total = refs
        narrow_at = where_ref[1]
        loads = weights.start(where_ref, pieces, held, sem)
        fetch = pltpu.make_async_copy(
            tokens_ref.at[pl.ds(pl.multiple_of(narrow_at * length, 16), length)], own, own_sem
        )
        fetch.start()
        allowed = same_segment(seg_ref[pl.ds(narrow_at, 1), :])
        grad = grad_ref[...]
        branch = grad.astype(BF16)
        branch_ref[...] = branch
        total[...] = jnp.zeros((length, width), F32)
        sums[...] = jnp.zeros(sums.shape, F32)
        for copies in loads:
            wait_all(copies)

        @pl.loop(0, parts)
        def _(z):
            context = mm_t(branch, held[z, 0, 3 * inner :]).astype(BF16)
            proj = qkv_ref[z]
            grads = [[], [], []]
            for h in range(heads):
                q, k, v = [proj[:, s * inner + h * HD : s * inner + (h + 1) * HD] for s in range(3)]
                up = context[:, h * HD : (h + 1) * HD]
                line = line_ref[z ^ narrow_at, h : h + 1]
                scores = mm_t(q, k) + toeplitz(line, length)[:, :length]
                probs = masked_softmax(scores, allowed)
                grad_probs = mm_t(up, v)
                delta = jnp.sum(grad_probs * probs, axis=-1, keepdims=True)
                grad_scores = (probs * (grad_probs - delta)).astype(BF16)
                sums[z, h : h + 1, :] = diagonal_sums(grad_scores, lanes)
                grads[0].append(mm(grad_scores, k).astype(BF16))
                grads[1].append(t_mm(grad_scores, q).astype(BF16))
                grads[2].append(t_mm(probs.astype(BF16), up).astype(BF16))
            dqkv = jnp.concatenate(grads[0] + grads[1] + grads[2], axis=1)
            dqkv_ref[z] = dqkv
            total[...] += mm(dqkv, held[z, 0, : 3 * inner])

        fetch.wait()
        pulled, gain = norm_back(total[...], own[...].astype(F32), gains_ref[0:1])
        out_ref[...] = (grad_ref[...] + pulled).astype(BF16)
        tables = [exact_mm(sums[z], buckets_ref[...]) for z in range(parts)]
        blank = jnp.zeros((8, width - parts * bucket_count), F32)
        first_rows = jnp.concatenate([gain, second_ref[...], known_ref[0:1], jnp.zeros((5, width), F32)], axis=0)
        shared_ref[...] = jnp.concatenate(
            [first_rows, jnp.concatenate(tables + [blank], axis=1)], axis=0
        )

    return call(
        kernel,
        "attention_backward",
        [smem(where), grad_hidden, *hidden_gains, qkv, anywhere(tokens), segments, gains, bias_line, buckets]
        + weights.inputs,
        [((length, width), BF16), (qkv.shape, BF16), ((length, width), BF16), ((16, width), F32)],
        weights.scratch
        + [
            pltpu.VMEM((length, width), BF16),
            pltpu.SemaphoreType.DMA,
            pltpu.VMEM((parts, 8, lanes), F32),
            pltpu.VMEM((length, width), F32),
        ],
        vmem=40,
        us=15,
    )


def decoder_weights(where, context, branch, normed, back, act, grad_output, inner):
    count, width = context.shape
    parts = width // inner

    def kernel(where_ref, ctx_ref, branch_ref, normed_ref, back_ref, act_ref, up_ref, outward_ref, grow_ref, shrink_ref):
        mine = jnp.zeros((count, inner), BF16)
        for z in range(parts):
            mine = jnp.where(where_ref[1] == z, ctx_ref[:, z * inner : (z + 1) * inner], mine)
        outward_ref[...] = t_mm(mine, branch_ref[...])
        grow_ref[...] = t_mm(normed_ref[...], back_ref[...])
        shrink_ref[...] = t_mm(act_ref[...], up_ref[...])

    return call(
        kernel,
        "decoder_weights",
        [smem(where), context, branch, normed, back, act, grad_output],
        [((inner, width), F32), ((width, back.shape[1]), F32), ((act.shape[1], width), F32)],
    )


def decoder_backward(
    where, query_sums, cross_weights, cross_normed, first, grad_second, gains, outward, inward, context,
    normed, proj, bias_line, buckets, answers,
):
    count, width = first.shape
    inner = outward.shape[0]
    heads = inner // HD
    parts = width // inner
    lanes, bucket_count = buckets.shape

    def kernel(where_ref, one_ref, two_ref, query_w_ref, cross_normed_ref, first_ref, grad_second_ref, gains_ref, *refs):
        outward_ref, inward_ref, ctx_ref, normed_ref, proj_ref, line_ref, buckets_ref = refs[:7]
        first_out, query_out, outward_out, inward_out, part_out, bias_out, gain_out, held, sem = refs[7:]
        fetch = fetch_rows(query_w_ref, 3 * inner, held, sem)
        grad_queries = (one_ref[...] + two_ref[...]).astype(BF16)
        mine = jnp.zeros((count, inner), BF16)
        total = jnp.zeros((count, width), F32)
        fetch.wait()
        for z in range(parts):
            block = grad_queries[:, z * inner : (z + 1) * inner]
            mine = jnp.where(where_ref[1] == z, block, mine)
            total = total + mm(block, held[z])
        query_out[...] = t_mm(mine, cross_normed_ref[...])
        pulled, gain = norm_back(total, first_ref[...], gains_ref[1:2])
        gain_out[...] = gain
        grad_first = grad_second_ref[...] + pulled
        first_out[...] = grad_first
        branch = grad_first.astype(BF16)
        outward_out[...] = t_mm(ctx_ref[...], branch)
        up_all = mm_t(branch, outward_ref[...]).astype(BF16)
        proj = proj_ref[...]
        allowed = causal_mask(count, answers)
        grads, bias_rows = [[], [], []], []
        for h in range(heads):
            q, k, v = [proj[:, s * inner + h * HD : s * inner + (h + 1) * HD] for s in range(3)]
            up = up_all[:, h * HD : (h + 1) * HD]
            scores = mm_t(q, k) + toeplitz(line_ref[h : h + 1], count)[:, :count]
            probs = masked_softmax(scores, allowed)
            grad_probs = mm_t(up, v)
            delta = jnp.sum(grad_probs * probs, axis=-1, keepdims=True)
            grad_scores = (probs * (grad_probs - delta)).astype(BF16)
            bias_rows.append(diagonal_sums(grad_scores, lanes))
            grads[0].append(mm(grad_scores, k).astype(BF16))
            grads[1].append(t_mm(grad_scores, q).astype(BF16))
            grads[2].append(t_mm(probs.astype(BF16), up).astype(BF16))
        dqkv = jnp.concatenate(grads[0] + grads[1] + grads[2], axis=1)
        inward_out[...] = t_mm(dqkv, normed_ref[...])
        part_out[...] = mm(dqkv, inward_ref[...])
        bias_out[...] = exact_mm(jnp.concatenate(bias_rows, axis=0), buckets_ref[...])

    return call(
        kernel,
        "decoder_backward",
        [
            smem(where),
            *query_sums,
            anywhere(cross_weights),
            cross_normed,
            first,
            grad_second,
            gains,
            outward,
            inward,
            context,
            normed,
            proj,
            bias_line,
            buckets,
        ],
        [
            ((count, width), F32),
            ((inner, width), F32),
            ((inner, width), F32),
            ((3 * inner, width), F32),
            ((count, width), F32),
            ((heads, bucket_count), F32),
            ((1, width), F32),
        ],
        [pltpu.VMEM((parts, inner, width), BF16), pltpu.SemaphoreType.DMA],
    )


def vocabulary_grads(where, ids, zero_sums, embedded, gains, grad_first, second, cross_gain, known_gains, rows):
    count, width = embedded.shape

    def kernel(where_ref, ids_ref, one_ref, two_ref, embedded_ref, gains_ref, first_ref, second_ref, *refs):
        cross_ref, known_ref, table_ref, output_ref, gain_ref, grads = refs
        sums = one_ref[...] + two_ref[...]
        output_ref[...] = (second_ref[...] + sums[count:]).astype(BF16)
        pulled, gain = norm_back(sums[:count], embedded_ref[...].astype(F32), gains_ref[0:1])
        gain_ref[...] = jnp.concatenate([gain, cross_ref[...], known_ref[1:2]], axis=0)
        grads[...] = first_ref[...] + pulled
        table_ref[...] = jnp.zeros(table_ref.shape, F32)
        base = where_ref[3] * rows

        @pl.loop(0, count)
        def _(i):
            local = ids_ref[i] - base

            @pl.when((local >= 0) & (local < rows))
            def _():
                table_ref[pl.ds(local, 1), :] += grads[pl.ds(i, 1), :]

    return call(
        kernel,
        "vocabulary_grads",
        [smem(where), smem(ids), *zero_sums, embedded, gains, grad_first, second, cross_gain, known_gains],
        [((rows, width), F32), ((count, width), BF16), ((3, width), F32)],
        [pltpu.VMEM((count, width), F32)],
        vmem=32,
    )


def both_bucket(offset):
    spread = np.abs(offset)
    far = 8 + sum((spread >= edge).astype(np.int32) for edge in BOTH_EDGES)
    return np.where(offset > 0, 16, 0) + np.where(spread < 8, spread, far)


def causal_bucket(offset):
    back = np.maximum(-offset, 0)
    far = 16 + sum((back >= edge).astype(np.int32) for edge in CAUSAL_EDGES)
    return np.where(back < 16, back, far)


def bucket_lines(bucket, count, buckets):
    lanes = 128
    while lanes < 2 * count:
        lanes *= 2
    place = np.arange(lanes)
    turning = bucket(np.where(place < lanes // 2, place, place - lanes))
    straight = bucket(place - (count - 1))
    rows = np.arange(buckets)
    return (
        (rows[:, None] == turning[None]).astype(np.float32),
        (straight[:, None] == rows[None]).astype(np.float32),
    )


def per_device(
    tokens,
    segments,
    question,
    answer_ids,
    vocab_table,
    enc_gains,
    enc_inward,
    encoder_bias,
    enc_outward,
    enc_grow,
    enc_shrink,
    cross_key_value_weight,
    dec_gains,
    dec_inward,
    decoder_bias,
    dec_outward,
    cross_query,
    cross_outward,
    dec_grow,
    dec_shrink,
    grad_memory,
    grad_output,
):
    parts = lax.axis_size("narrow")
    narrow_at = lax.axis_index("narrow")
    bits, slab = slab_bits()
    low = bits[0]
    length = segments.shape[1]
    width = tokens.shape[1]
    inner = enc_outward.shape[0]
    heads = inner // HD
    questions, answers = answer_ids.shape
    count = questions * answers
    ids = answer_ids.reshape(-1)
    own_question = lax.dynamic_index_in_dim(question, narrow_at, 0, keepdims=False)
    where = jnp.stack([slab, narrow_at, own_question, lax.axis_index("wide")]).astype(I32)

    def turned(weight):
        return jnp.transpose(weight, (1, 2, 0)).reshape(-1, width)

    enc_in, dec_in, cross_kv = turned(enc_inward), turned(dec_inward), turned(cross_key_value_weight)
    cross_q = cross_query.T

    def own_slab(*matrices):
        whole = matrices[0] if len(matrices) == 1 else jnp.concatenate(matrices)
        rows = whole.shape[0] // SLABS
        return lax.dynamic_slice_in_dim(whole, slab * rows, rows, 0)

    attn_pieces = gather_pieces(own_slab(enc_in, enc_outward))
    ffn_pieces = gather_pieces(jnp.concatenate([own_slab(enc_shrink), own_slab(enc_grow)]))
    cross_pieces = gather_pieces(own_slab(cross_kv, cross_outward, cross_q))
    attn_weights = Weights([(enc_in, 0, 0), (enc_outward, 0, 3 * inner)], attn_pieces, parts)
    ffn_weights = Weights([(enc_shrink, 0, 0), (enc_grow, 1, 0)], ffn_pieces, parts)
    cross_weights = Weights(
        [(cross_kv, 0, 0), (cross_outward, 0, 2 * inner), (cross_q, 0, 3 * inner)], cross_pieces, parts
    )

    table = encoder_bias.T
    tables = jnp.stack([table] + [swap(table, "narrow", offset) for offset in range(1, parts)])
    both, both_sums = bucket_lines(both_bucket, length, table.shape[1])
    causal, causal_sums = bucket_lines(causal_bucket, count, table.shape[1])
    enc_line = jnp.einsum("zhb,bt->zht", tables, both, precision=FULL)
    dec_line = jnp.einsum("bh,bt->ht", decoder_bias, causal, precision=FULL)

    vocab_local = vocab_table.shape[0]
    if vocab_local % 16 == 0:
        embedded = embed_rows(where, ids, vocab_table)
    else:
        local_ids = where[3] * vocab_local + jnp.arange(vocab_local, dtype=I32)
        one_hot = (ids[:, None] == local_ids[None, :]).astype(BF16)
        embedded = jnp.dot(one_hot, vocab_table, preferred_element_type=F32).astype(BF16)
    embedded = exchange_sum(embedded, "wide")
    dec_normed, dec_proj, dec_context, self_part = decoder_self(
        embedded, dec_gains, dec_in, dec_outward, dec_line, answers
    )
    self_sums = exchange_pair(self_part, "narrow")

    hidden, first_normed, qkv, context = encoder_attention(
        where, tokens, segments, enc_gains, enc_line, attn_weights
    )
    second_normed, act, slope, summed, memory = encoder_ffn(where, hidden, enc_gains, ffn_weights)

    dec_first, cross_normed, queries, kv, stats, cross_all = cross_forward(
        where, memory, embedded, self_sums, dec_gains, cross_weights, answers, inner
    )
    steps = [("wide", bit) for bit in bits_of(lax.axis_size("wide"))]
    steps += [("narrow", bit) for bit in bits_of(parts)]
    for axis, bit in steps[:-1]:
        stats = merge_stats(stats, swap(stats, axis, bit))
    exact, stats, cross_context, dec_second, third_normed, dec_act, dec_back, third_part, output_part = decoder_middle(
        stats, swap(stats, *steps[-1]), dec_first, cross_all, dec_gains, dec_grow, dec_shrink, grad_output, inner
    )
    third_sums = exchange_pair(third_part, "narrow")
    grad_dec_second, cross_branch, grad_kv, query_part, grad_summed, ffn_branch, known_gains = cross_backward(
        where, third_sums, dec_second, dec_gains, grad_output, cross_all, kv, queries, stats, exact,
        grad_memory, summed, enc_gains, answers,
    )

    sent_early = scatter_sums(*weight_grads(where, [(ffn_branch, act), (memory, grad_kv)], "shrink_weight_grads"))
    grad_grown, grad_hidden, second_gain = ffn_backward(
        where, grad_summed, slope, hidden, enc_gains, ffn_weights
    )
    sent_grow = scatter_sums(*weight_grads(where, [(second_normed, grad_grown)], "grow_weight_grads"))
    attn_branch, grad_qkv, own_grad_tokens, shared = attention_backward(
        where, grad_hidden, (known_gains, second_gain), first_normed, qkv, tokens, segments, enc_gains,
        enc_line, jnp.asarray(both_sums), attn_weights,
    )
    sent_attn = scatter_sums(
        *weight_grads(where, [(first_normed, grad_qkv), (attn_branch, context)], "attention_weight_grads")
    )
    grad_tokens = spread_rows(own_grad_tokens)
    memory_out = spread_rows(memory)
    shared = exchange_sum(exchange_sum(shared, "wide"), "narrow")

    grad_cross_outward, grad_dec_grow, grad_dec_shrink = decoder_weights(
        where, cross_context, cross_branch, third_normed, dec_back, dec_act, grad_output, inner
    )
    query_sums = exchange_pair(exchange_sum(query_part, "wide"), "narrow")
    grad_dec_first, grad_cross_q, grad_dec_outward, grad_dec_in, zero_part, dec_bias_grads, cross_gain = decoder_backward(
        where, query_sums, cross_all, cross_normed, dec_first, grad_dec_second, dec_gains, dec_outward, dec_in,
        dec_context, dec_normed, dec_proj, dec_line, jnp.asarray(causal_sums), answers,
    )
    zero_sums = exchange_pair(jnp.concatenate([zero_part, output_part]), "narrow")
    grad_vocab_table, output, grad_dec_gains = vocabulary_grads(
        where, ids, zero_sums, embedded, dec_gains, grad_dec_first, dec_second, cross_gain, known_gains, vocab_local
    )

    units = enc_grow.shape[1]
    sent_shrink, sent_cross = sent_early[:, :units], sent_early[:, units:]
    own_bias = lax.dynamic_slice(shared, (8, narrow_at * table.shape[1]), (heads, table.shape[1]))
    rows = sent_attn.shape[0]
    return (
        memory_out,
        output,
        grad_tokens,
        grad_vocab_table,
        shared[:3],
        sent_attn[:, : 3 * inner].reshape(rows, 3, inner),
        own_bias.T,
        sent_attn[:, 3 * inner :].T,
        sent_grow,
        sent_shrink.T,
        sent_cross.reshape(rows, 2, inner),
        grad_dec_gains,
        jnp.transpose(grad_dec_in.reshape(3, inner, width), (2, 0, 1)),
        dec_bias_grads.T,
        grad_dec_outward,
        grad_cross_q.T,
        grad_cross_outward,
        grad_dec_grow,
        grad_dec_shrink,
    )


def solution(mesh):
    in_specs = (
        P("wide", None),
        P("wide", None),
        P("wide"),
        P(),
        P("wide", None),
        P(),
        P(None, None, "narrow"),
        P(None, "narrow"),
        P("narrow", None),
        P(None, "narrow"),
        P("narrow", None),
        P(None, None, "narrow"),
        P(),
        P(None, None, "narrow"),
        P(None, "narrow"),
        P("narrow", None),
        P(None, "narrow"),
        P("narrow", None),
        P(None, "narrow"),
        P("narrow", None),
        P("wide", None),
        P(),
    )
    out_specs = (
        P("wide", None),
        P(),
        P("wide", None),
        P("wide", None),
        P(),
        P("wide", None, "narrow"),
        P(None, "narrow"),
        P("narrow", "wide"),
        P("wide", "narrow"),
        P("narrow", "wide"),
        P("wide", None, "narrow"),
        P(),
        P(None, None, "narrow"),
        P(None, "narrow"),
        P("narrow", None),
        P(None, "narrow"),
        P("narrow", None),
        P(None, "narrow"),
        P("narrow", None),
    )
    return jax.shard_map(
        per_device, mesh=mesh, in_specs=in_specs, out_specs=out_specs, check_vma=False
    )
```
